512 devices in a mesh: dp: 64 (over x, y, core), shard: 8 (over z).
Axes of the slice: x: 4, y: 8, z: 8, core: 2. Of those that a mesh axis runs over, the one named last changes fastest.
Arguments:
- grads: bfloat16 [8, 4096, 512], P('shard', 'dp')
- left_old: float32 [8, 4096, 512], P('shard', 'dp'), as said below
- right_old: float32 [8, 4096, 512], P('shard', 'dp'), as said below
- root_steps: int32 [8, 8, 2], P('shard'), may hold values from 1 to 3, as said below
Outputs:
- update: bfloat16 [8, 4096, 512], P('shard')
- left_new: float32 [8, 4096, 512], P('shard', 'dp')
- right_new: float32 [8, 4096, 512], P('shard', 'dp')
The draws below stay inside these ranges and needn't reach their ends.
Inputs may be any that keep to these rules, and one draw needn't show every extreme that they name: `root_steps`: every entry is 1, 2 or 3; in every draw some entry is 1 and some entry is 3. `left_old`: every block is symmetric and positive definite. `right_old`: every block is symmetric and positive definite.
All inputs are finite; a program needn't handle non-finite values.
Results may differ from the reference program's by a relative error of at most 0.0045.
Values may be sent and summed in bfloat16 or wider, within the bound.
No kernel may reach another device: no remote copies, remote signals or barrier semaphores. Data moves between devices by JAX's collectives and lax.ppermute only.
A program may use at most 64 MiB of HBM per device.

```python
import math
import jax
import jax.numpy as jnp
from jax import lax

ORDER = 512
STEPS = 3
STACK_BLOCKS = 8
SHARDS = 8
SPAN = 4096


def grad_scales(key):
    keys = jax.random.split(key, 2)
    row_scale = jnp.exp(jax.random.uniform(keys[0], (SHARDS, SPAN, 1), jnp.float32, 0.0, math.log(10.0)))
    col_scale = jnp.exp(jax.random.uniform(keys[1], (SHARDS, 1, ORDER), jnp.float32, 0.0, math.log(3.0)))
    return (row_scale, col_scale)


def factor_blocks(vectors, exponent, edge_scale, strength):
    vectors = vectors / math.sqrt(ORDER)
    rank_index = jnp.arange(1, ORDER + 1).astype(jnp.float32)
    spectrum = rank_index ** (-exponent)
    kernel = jnp.einsum('sbik,sbjk->sbij', vectors * spectrum, vectors, precision=lax.Precision.HIGHEST)
    identity = (jnp.arange(ORDER)[:, None] == jnp.arange(ORDER)[None, :]).astype(jnp.float32)
    scaled = edge_scale * kernel * jnp.swapaxes(edge_scale, 2, 3) + 0.02 * identity
    symmetric = 0.5 * (scaled + jnp.swapaxes(scaled, 2, 3))
    return (strength * symmetric).reshape(SHARDS, SPAN, ORDER)


def draw_left_old(key, part):
    row_scale = grad_scales(key)[0]
    key = jax.random.fold_in(key, 5)
    shape = (SHARDS, STACK_BLOCKS, ORDER, ORDER)
    vectors = jax.random.normal(key, shape, jnp.float32)
    exponent = 0.8
    edge_scale = row_scale.reshape(SHARDS, STACK_BLOCKS, ORDER, 1)
    return factor_blocks(vectors, exponent, edge_scale, 4.0 * ORDER)


def draw_right_old(key, part):
    col_scale = grad_scales(key)[1]
    key = jax.random.fold_in(key, 7)
    shape = (SHARDS, STACK_BLOCKS, ORDER, ORDER)
    vectors = jax.random.normal(key, shape, jnp.float32)
    exponent = 0.8
    edge_scale = col_scale.reshape(SHARDS, 1, ORDER, 1)
    return factor_blocks(vectors, exponent, edge_scale, 16.0 * ORDER)


def draw_grads(key, part):
    row_scale, col_scale = grad_scales(key)
    key = jax.random.fold_in(key, 11)
    keys = jax.random.split(key, 1)
    shape = (SHARDS, SPAN, ORDER)
    noise = jax.random.normal(keys[0], shape, jnp.float32)
    block_index = (jnp.arange(SPAN) // ORDER).astype(jnp.float32)
    fraction = block_index / max(STACK_BLOCKS - 1, 1)
    rising = jnp.sqrt(1.0 + 2.0 * fraction)[None, :, None]
    return (noise * row_scale * col_scale * rising / 6.0).astype(jnp.bfloat16)


def draw_root_steps(key, part):
    key = jax.random.fold_in(key, 29)
    keys = jax.random.split(key, 3)
    total = SHARDS * STACK_BLOCKS * 2
    level_draw = jax.random.randint(keys[0], (total,), 0, 10)
    counts = jnp.where(level_draw < 6, 1, jnp.where(level_draw < 8, 2, STEPS)).astype(jnp.int32)
    first_spot = jax.random.randint(keys[1], (), 0, total)
    second_spot = (first_spot + 1 + jax.random.randint(keys[2], (), 0, total - 1)) % total
    counts = counts.at[first_spot].set(STEPS).at[second_spot].set(1)
    return counts.reshape(SHARDS, STACK_BLOCKS, 2).astype(jnp.int32)


def setup_inputs(seed: int = 0) -> dict:
    arg_keys = jax.random.split(jax.random.key(seed), 5)
    return {
        "grads": draw_grads(jax.random.fold_in(arg_keys[4], 71), 0),
        "left_old": draw_left_old(jax.random.fold_in(arg_keys[4], 71), 0),
        "right_old": draw_right_old(jax.random.fold_in(arg_keys[4], 71), 0),
        "root_steps": draw_root_steps(jax.random.fold_in(arg_keys[4], 71), 0),
    }


epsilon = 1e-06
decay_rate = 0.95

def precise_dot(left, right):
    return jnp.dot(left, right, precision=lax.Precision.HIGHEST, preferred_element_type=jnp.float32)

def inverse_root(factor, step_count):
    identity = jnp.eye(factor.shape[0], dtype=jnp.float32)
    magnitude = jnp.sqrt(jnp.sum(factor * factor) + epsilon)
    scaling = 2.5 / magnitude

    def newton(iteration, carry_pair):
        matrix, inverse = carry_pair
        shifted = (5.0 * identity - matrix) * 0.25
        new_inverse = precise_dot(inverse, shifted)
        square = precise_dot(shifted, shifted)
        fourth = precise_dot(square, square)
        new_matrix = precise_dot(fourth, matrix)
        active = iteration < step_count
        return (jnp.where(active, new_matrix, matrix), jnp.where(active, new_inverse, inverse))
    start_pair = (scaling * factor, jnp.sqrt(jnp.sqrt(scaling)) * identity)
    return lax.fori_loop(0, STEPS, newton, start_pair)[1]

def reference(grads, left_old, right_old, root_steps):
    total = SHARDS * STACK_BLOCKS
    grad_blocks = grads.reshape(total, ORDER, ORDER)
    left_blocks = left_old.reshape(total, ORDER, ORDER)
    right_blocks = right_old.reshape(total, ORDER, ORDER)
    count_pairs = root_steps.reshape(total, 2)

    def one_block(inputs):
        grad_block, left_block, right_block, counts = inputs
        left_fresh = decay_rate * left_block + jnp.dot(grad_block, grad_block.T, preferred_element_type=jnp.float32)
        right_fresh = decay_rate * right_block + jnp.dot(grad_block.T, grad_block, preferred_element_type=jnp.float32)
        left_root = inverse_root(left_fresh, counts[0])
        right_root = inverse_root(right_fresh, counts[1])
        conditioned = precise_dot(precise_dot(left_root, grad_block.astype(jnp.float32)), right_root)
        return (left_fresh, right_fresh, conditioned)
    left_fresh, right_fresh, conditioned = lax.map(one_block, (grad_blocks, left_blocks, right_blocks, count_pairs))
    grad_square = jnp.sum(jnp.square(grads.astype(jnp.float32)))
    cond_square = jnp.sum(conditioned * conditioned)
    graft_ratio = jnp.sqrt(grad_square / (cond_square + epsilon))
    update = (conditioned * graft_ratio).astype(jnp.bfloat16).reshape(SHARDS, SPAN, ORDER)
    return (update, left_fresh.reshape(SHARDS, SPAN, ORDER), right_fresh.reshape(SHARDS, SPAN, ORDER))
```

```python
import jax
import jax.numpy as jnp
from jax import lax
from jax.experimental import pallas as pl
from jax.experimental.pallas import tpu as pltpu
from jax.sharding import PartitionSpec as P

GROUP = 8
SLAB = 64
ORDER = 512
HALF = ORDER // 2

epsilon = 1e-06
decay_rate = 0.95


def flipped(value, axis, mask):
    return lax.ppermute(value, axis, [(i, i ^ mask) for i in range(lax.axis_size(axis))])


def dot(left, right, dims=((1,), (0,))):
    return lax.dot_general(left, right, (dims, ((), ())), preferred_element_type=jnp.float32)


def short(value):
    return value.astype(jnp.bfloat16)


def refresh_kernel(scalars, *refs):
    pieces = refs[:8]
    left_own, right_own, left_out, right_out, cond_out, sums_out = refs[8:14]
    grad, old_left, old_right, work, poly, total = refs[14:]
    member = scalars[0]
    for relative, piece in enumerate(pieces):
        rows = pl.ds(pl.multiple_of((member ^ relative) * SLAB, SLAB), SLAB)
        grad[rows, :] = piece[0:SLAB, :]
        old_left[rows, :] = piece[SLAB : 2 * SLAB, :]
        old_right[rows, :] = piece[2 * SLAB :, :]
    own = pl.ds(pl.multiple_of(member * SLAB, SLAB), SLAB)

    def start(old, own_old, out, dims):
        work[...] = dot(grad[...], grad[...], dims)
        out[...] = decay_rate * own_old[...] + work[own, :]
        factor = work[...] + decay_rate * old[...].astype(jnp.float32)
        scaling = 2.5 / jnp.sqrt(jnp.sum(factor * factor, keepdims=True) + epsilon)
        work[...] = factor * (scaling * 0.25)
        return jnp.sqrt(jnp.sqrt(scaling))

    def advance():
        quarter = work[...]
        low = short(quarter)
        poly[...] = 2.5 * quarter - dot(low, low)
        low_square = short(poly[...])
        fourth = 3.125 * poly[...] - dot(low_square, low_square)
        work[...] = 2.44140625 * quarter - dot(short(fourth), low)

    def apply_left():
        total[...] = 1.25 * total[...] - dot(short(work[...]), short(total[...]))

    def apply_right():
        total[...] = 1.25 * total[...] - dot(short(total[...]), short(work[...]))

    def chain(count, apply):
        apply()

        @pl.when(count > 1)
        def _():
            advance()
            apply()

        @pl.when(count > 2)
        def _():
            advance()
            apply()

    total[...] = grad[...].astype(jnp.float32)
    grad_square = jnp.sum(total[...] * total[...], keepdims=True)
    left_scale = start(old_left, left_own, left_out, ((1,), (1,)))
    chain(scalars[1], apply_left)
    right_scale = start(old_right, right_own, right_out, ((0,), (0,)))
    chain(scalars[2], apply_right)
    conditioned = total[...] * (left_scale * right_scale)
    cond_out[...] = short(conditioned)
    sums_out[0:4, :] = jnp.broadcast_to(jnp.sum(conditioned * conditioned, keepdims=True), (4, 128))
    sums_out[4:8, :] = jnp.broadcast_to(grad_square, (4, 128))


def refresh(scalars, pieces, left_own, right_own):
    vmem = pl.BlockSpec(memory_space=pltpu.VMEM)
    full = (ORDER, ORDER)
    return pl.pallas_call(
        refresh_kernel,
        out_shape=(
            jax.ShapeDtypeStruct((SLAB, ORDER), jnp.float32),
            jax.ShapeDtypeStruct((SLAB, ORDER), jnp.float32),
            jax.ShapeDtypeStruct(full, jnp.bfloat16),
            jax.ShapeDtypeStruct((8, 128), jnp.float32),
        ),
        in_specs=[pl.BlockSpec(memory_space=pltpu.SMEM)] + [vmem] * 10,
        out_specs=(vmem,) * 4,
        scratch_shapes=[pltpu.VMEM(full, jnp.bfloat16)] * 3 + [pltpu.VMEM(full, jnp.float32)] * 3,
        compiler_params=pltpu.CompilerParams(vmem_limit_bytes=40 * 1024 * 1024),
        name="refresh",
    )(scalars, *pieces, left_own, right_own)


def place_kernel(scalars, ratio, *refs):
    sources, out = refs[:4], refs[4]
    for relative, source in enumerate(sources):
        place = scalars[0] ^ relative
        rows = pl.ds(pl.multiple_of(place * HALF, HALF), HALF)
        out[rows, :] = short(source[0].astype(jnp.float32) * ratio[0:1, 0:1])


def place(scalars, ratio, sources):
    columns = 4
    piece = pl.BlockSpec((1, HALF, ORDER), lambda i: (i, 0, 0))
    return pl.pallas_call(
        place_kernel,
        out_shape=jax.ShapeDtypeStruct((columns * 2 * ORDER, ORDER), jnp.bfloat16),
        grid=(columns,),
        in_specs=[pl.BlockSpec(memory_space=pltpu.SMEM), pl.BlockSpec((8, 128), lambda i: (0, 0))]
        + [piece] * 4,
        out_specs=pl.BlockSpec((2 * ORDER, ORDER), lambda i: (i, 0)),
        compiler_params=pltpu.CompilerParams(vmem_limit_bytes=40 * 1024 * 1024),
        name="place",
    )(scalars, ratio, *sources)


def per_device(grads, left_old, right_old, root_steps):
    position = lax.axis_index("dp")
    member = position % GROUP
    block = position // GROUP
    core = position % 2
    own = jnp.concatenate([grads[0], short(left_old[0]), short(right_old[0])], axis=0)
    far = flipped(own, "dp", 4)
    near = flipped(own, "dp", 2)
    both = flipped(far, "dp", 2)
    pieces = [None] * 8
    for relative, piece in ((0, own), (2, near), (4, far), (6, both)):
        pieces[relative] = piece
        pieces[relative + 1] = flipped(piece, "dp", 1)
    counts = lax.dynamic_index_in_dim(root_steps[0], block, 0, keepdims=False)
    scalars = jnp.stack([member, counts[0], counts[1]])
    left_rows, right_rows, conditioned, sums = refresh(scalars, pieces, left_old[0], right_old[0])

    columns = [[16 * i + k for i in range(4)] for k in range(16)]

    def to_columns(value):
        copies = jnp.broadcast_to(value[None], (4, *value.shape))
        return lax.all_to_all(copies, "dp", 0, 0, axis_index_groups=columns)

    half = lax.dynamic_slice_in_dim(conditioned, core * HALF, HALF, 0)
    mirrored = flipped(half, "dp", 14)
    same = to_columns(half)
    cross = to_columns(mirrored)
    same_other = flipped(same, "dp", 1)
    cross_other = flipped(cross, "dp", 1)

    stacks = lax.all_to_all(jnp.broadcast_to(sums[None], (8, 8, 128)), "shard", 0, 0)
    sums = jnp.sum(stacks, axis=0)
    sums = sums + flipped(sums, "dp", 14)
    sums = jnp.sum(to_columns(sums), axis=0)
    ratio = jnp.sqrt(sums[4:5] / (sums[0:1] + epsilon))
    ratio = jnp.broadcast_to(ratio, (8, 128))

    slot = (block % 2) * 2 + core
    update = place(
        jnp.reshape(slot, (1,)), ratio, [same, same_other, cross, cross_other]
    )
    return (update[None], left_rows[None], right_rows[None])


def solution(mesh):
    placed = (
        P("shard", "dp", None),
        P("shard", "dp", None),
        P("shard", "dp", None),
        P("shard", None, None),
    )
    return jax.shard_map(
        per_device,
        mesh=mesh,
        in_specs=placed,
        out_specs=(P("shard", None, None), P("shard", "dp", None), P("shard", "dp", None)),
        check_vma=False,
    )
```

```python
import jax
import jax.numpy as jnp
from jax import lax
from jax.experimental import pallas as pl
from jax.experimental.pallas import tpu as pltpu
from jax.sharding import PartitionSpec as P

GROUP = 8
SLAB = 64
ORDER = 512
HALF = ORDER // 2
SENT = HALF + 16
PANEL = 256
COLUMNS = 4

epsilon = 1e-06
decay_rate = 0.95

VMEM = pl.BlockSpec(memory_space=pltpu.VMEM)
SMEM = pl.BlockSpec(memory_space=pltpu.SMEM)
HBM = pl.BlockSpec(memory_space=pltpu.HBM)
PARAMS = pltpu.CompilerParams(vmem_limit_bytes=16 * 1024 * 1024)


def flipped(value, axis, mask):
    return lax.ppermute(value, axis, [(i, i ^ mask) for i in range(lax.axis_size(axis))])


def dot(left, right, dims=((1,), (0,))):
    return lax.dot_general(left, right, (dims, ((), ())), preferred_element_type=jnp.float32)


def short(value):
    return value.astype(jnp.bfloat16)


def thirds(value):
    parts = []
    for _ in range(3):
        parts.append(jnp.broadcast_to(short(value), (1, ORDER)))
        value = value - short(value).astype(jnp.float32)
    return parts


def refresh_kernel(position, steps, *refs):
    pieces = refs[:8]
    products_out, half_out, copies_out = refs[8:11]
    grad, old_left, old_right, low, low_square, fourth, short_total, work, poly, total = refs[11:]
    member = position[0] & (GROUP - 1)
    block = position[0] // GROUP
    for relative, piece in enumerate(pieces):
        rows = pl.ds(pl.multiple_of((member ^ relative) * SLAB, SLAB), SLAB)
        grad[rows, :] = piece[0:SLAB, :]
        old_left[rows, :] = piece[SLAB : 2 * SLAB, :]
        old_right[rows, :] = piece[2 * SLAB :, :]
    own = pl.ds(pl.multiple_of(member * SLAB, SLAB), SLAB)

    panels = [pl.ds(row, PANEL) for row in range(0, ORDER, PANEL)]

    def start(side, old, dims):
        square = jnp.zeros((1, 1), jnp.float32)
        for rows in panels:
            if side == 0:
                product = dot(grad[rows, :], grad[...], dims)
            else:
                product = dot(grad[:, rows], grad[...], dims)
            work[rows, :] = product
            factor = product + decay_rate * old[rows, :].astype(jnp.float32)
            poly[rows, :] = factor
            square = square + jnp.sum(factor * factor, keepdims=True)
        products_out[side] = work[own, :]
        scaling = 2.5 / jnp.sqrt(square + epsilon)
        for rows in panels:
            quarter = poly[rows, :] * (scaling * 0.25)
            work[rows, :] = quarter
            low[rows, :] = short(quarter)
        return jnp.sqrt(jnp.sqrt(scaling))

    def advance():
        for rows in panels:
            partial = 2.5 * work[rows, :] - dot(low[rows, :], low[...])
            poly[rows, :] = partial
            low_square[rows, :] = short(partial)
        for rows in panels:
            fourth[rows, :] = short(
                3.125 * poly[rows, :] - dot(low_square[rows, :], low_square[...])
            )
        for rows in panels:
            work[rows, :] = 2.44140625 * work[rows, :] - dot(fourth[rows, :], low[...])
        for rows in panels:
            low[rows, :] = short(work[rows, :])

    def apply_left():
        for rows in panels:
            total[rows, :] = 1.25 * total[rows, :] - dot(low[rows, :], short_total[...])
        for rows in panels:
            short_total[rows, :] = short(total[rows, :])

    def apply_right():
        for rows in panels:
            value = 1.25 * total[rows, :] - dot(short_total[rows, :], low[...])
            total[rows, :] = value
            short_total[rows, :] = short(value)

    def chain(count, apply):
        apply()

        @pl.when(count > 1)
        def _():
            advance()
            apply()

        @pl.when(count > 2)
        def _():
            advance()
            apply()

    left_scale = start(0, old_left, ((1,), (1,)))
    grad_square = jnp.zeros((1, 1), jnp.float32)
    for rows in panels:
        value = grad[rows, :].astype(jnp.float32)
        total[rows, :] = value
        grad_square = grad_square + jnp.sum(value * value, keepdims=True)
        short_total[rows, :] = grad[rows, :]
    chain(steps[2 * block], apply_left)
    right_scale = start(1, old_right, ((0,), (0,)))
    chain(steps[2 * block + 1], apply_right)
    cond_square = jnp.zeros((1, 1), jnp.float32)
    for rows in panels:
        value = total[rows, :] * (left_scale * right_scale)
        total[rows, :] = value
        cond_square = cond_square + jnp.sum(value * value, keepdims=True)
    half = short(total[pl.ds(pl.multiple_of((member & 1) * HALF, HALF), HALF), :])
    half_out[0:HALF, :] = half
    half_out[HALF:, :] = jnp.concatenate(
        thirds(cond_square) + thirds(grad_square) + [jnp.zeros((10, ORDER), jnp.bfloat16)], axis=0
    )
    for column in range(COLUMNS):
        copies_out[column] = half_out[...]


def refresh(position, steps, pieces):
    full = (ORDER, ORDER)
    return pl.pallas_call(
        refresh_kernel,
        out_shape=(
            jax.ShapeDtypeStruct((2, SLAB, ORDER), jnp.float32),
            jax.ShapeDtypeStruct((SENT, ORDER), jnp.bfloat16),
            jax.ShapeDtypeStruct((COLUMNS, SENT, ORDER), jnp.bfloat16),
        ),
        in_specs=[SMEM] * 2 + [VMEM] * 8,
        out_specs=(VMEM,) * 3,
        scratch_shapes=[pltpu.VMEM(full, jnp.bfloat16)] * 7 + [pltpu.VMEM(full, jnp.float32)] * 3,
        compiler_params=PARAMS,
        name="refresh",
    )(position, steps, *pieces)


def spread_kernel(half, out):
    for column in range(COLUMNS):
        out[column] = half[...]


def spread(half):
    return pl.pallas_call(
        spread_kernel,
        out_shape=jax.ShapeDtypeStruct((COLUMNS, *half.shape), half.dtype),
        in_specs=[VMEM],
        out_specs=VMEM,
        compiler_params=PARAMS,
        name="spread",
    )(half)


def place_kernel(position, sums, *refs):
    sources, out, staged, sems = refs[:4], refs[4], refs[5], refs[6]
    squares = [sums[i : i + 1] + sums[i + 1 : i + 2] + sums[i + 2 : i + 3] for i in (0, 3)]
    ratio = jnp.sqrt(squares[1] / (squares[0] + epsilon))[:, 0:1]
    slot = ((position[0] // GROUP) & 1) * 2 + (position[0] & 1)
    stores = []
    for relative, source in enumerate(sources):
        for column in range(COLUMNS):
            index = relative * COLUMNS + column
            staged[index] = short(source[column, 0:HALF].astype(jnp.float32) * ratio)
            row = (column * 4 + (slot ^ relative)) * HALF
            rows = pl.ds(pl.multiple_of(row, HALF), HALF)
            store = pltpu.make_async_copy(staged.at[index], out.at[0, rows], sems.at[index])
            store.start()
            stores.append(store)
    for store in stores:
        store.wait()


def place(position, sums, sources):
    return pl.pallas_call(
        place_kernel,
        out_shape=jax.ShapeDtypeStruct((1, 4 * COLUMNS * HALF, ORDER), jnp.bfloat16),
        in_specs=[SMEM] + [VMEM] * 5,
        out_specs=HBM,
        scratch_shapes=[
            pltpu.VMEM((4 * COLUMNS, HALF, ORDER), jnp.bfloat16),
            pltpu.SemaphoreType.DMA((4 * COLUMNS,)),
        ],
        compiler_params=PARAMS,
        name="place",
    )(position, sums, *sources)


def tally(blocks):
    return jnp.sum(blocks[:, HALF : HALF + 8, 0:128].astype(jnp.float32), axis=0)


def per_device(grads, left_old, right_old, root_steps):
    position = jnp.reshape(lax.axis_index("dp"), (1,))
    steps = jnp.reshape(root_steps, (16,))
    own = short(jnp.concatenate([grads[0].astype(jnp.float32), left_old[0], right_old[0]], axis=0))
    far = flipped(own, "dp", 4)
    near = flipped(own, "dp", 2)
    far, steps = lax.optimization_barrier((far, steps))
    both = flipped(far, "dp", 2)
    pieces = [None] * 8
    for relative, piece in ((0, own), (2, near), (4, far), (6, both)):
        pieces[relative] = piece
        pieces[relative + 1] = flipped(piece, "dp", 1)
    products, half, copies = refresh(position, steps, pieces)
    left_rows = decay_rate * left_old + products[0:1]
    right_rows = decay_rate * right_old + products[1:2]

    columns = [[16 * i + k for i in range(COLUMNS)] for k in range(16)]
    mirrored = flipped(half, "dp", 14)
    same = lax.all_to_all(copies, "dp", 0, 0, axis_index_groups=columns)
    sums = tally(same)
    sums = sums + flipped(sums, "shard", 1)
    mirrored, sums, left_rows, right_rows = lax.optimization_barrier(
        (mirrored, sums, left_rows, right_rows)
    )
    mirrored = spread(mirrored)
    cross = lax.all_to_all(mirrored, "dp", 0, 0, axis_index_groups=columns)
    same_other = flipped(same, "dp", 1)
    for mask in (7, 2):
        sums = sums + flipped(sums, "shard", mask)
    cross, sums = lax.optimization_barrier((cross, sums))
    cross_other = flipped(cross, "dp", 1)
    sums = sums + flipped(sums, "dp", 14)
    update = place(position, sums, [same, same_other, cross, cross_other])
    return (update, left_rows, right_rows)


def solution(mesh):
    placed = (
        P("shard", "dp", None),
        P("shard", "dp", None),
        P("shard", "dp", None),
        P("shard", None, None),
    )
    return jax.shard_map(
        per_device,
        mesh=mesh,
        in_specs=placed,
        out_specs=(P("shard", None, None), P("shard", "dp", None), P("shard", "dp", None)),
        check_vma=False,
    )
```

```python
import jax
import jax.numpy as jnp
from jax import lax
from jax.experimental import pallas as pl
from jax.experimental.pallas import tpu as pltpu
from jax.sharding import PartitionSpec as P

GROUP = 8
SLAB = 64
ORDER = 512
HALF = ORDER // 2
PANEL = 256
COLUMNS = 4

epsilon = 1e-06
decay_rate = 0.95

VMEM = pl.BlockSpec(memory_space=pltpu.VMEM)
SMEM = pl.BlockSpec(memory_space=pltpu.SMEM)
HBM = pl.BlockSpec(memory_space=pltpu.HBM)
PARAMS = pltpu.CompilerParams(vmem_limit_bytes=16 * 1024 * 1024)


def flipped(value, axis, mask):
    return lax.ppermute(value, axis, [(i, i ^ mask) for i in range(lax.axis_size(axis))])


def dot(left, right, dims=((1,), (0,))):
    return lax.dot_general(left, right, (dims, ((), ())), preferred_element_type=jnp.float32)


def short(value):
    return value.astype(jnp.bfloat16)


def refresh_kernel(position, steps, *refs):
    pieces = refs[:8]
    products_out, half_out, sums_out = refs[8:11]
    grad, old_left, old_right, low, low_square, fourth, short_total, work, poly, total = refs[11:]
    member = position[0] & (GROUP - 1)
    block = position[0] // GROUP
    for relative, piece in enumerate(pieces):
        rows = pl.ds(pl.multiple_of((member ^ relative) * SLAB, SLAB), SLAB)
        grad[rows, :] = piece[0:SLAB, :]
        old_left[rows, :] = piece[SLAB : 2 * SLAB, :]
        old_right[rows, :] = piece[2 * SLAB :, :]
    own = pl.ds(pl.multiple_of(member * SLAB, SLAB), SLAB)

    panels = [pl.ds(row, PANEL) for row in range(0, ORDER, PANEL)]

    def start(side, old, dims):
        square = jnp.zeros((1, 1), jnp.float32)
        for rows in panels:
            if side == 0:
                product = dot(grad[rows, :], grad[...], dims)
            else:
                product = dot(grad[:, rows], grad[...], dims)
            work[rows, :] = product
            factor = product + decay_rate * old[rows, :].astype(jnp.float32)
            poly[rows, :] = factor
            square = square + jnp.sum(factor * factor, keepdims=True)
        products_out[side] = work[own, :]
        scaling = 2.5 / jnp.sqrt(square + epsilon)
        for rows in panels:
            quarter = poly[rows, :] * (scaling * 0.25)
            work[rows, :] = quarter
            low[rows, :] = short(quarter)
        return jnp.sqrt(jnp.sqrt(scaling))

    def advance():
        for rows in panels:
            partial = 2.5 * work[rows, :] - dot(low[rows, :], low[...])
            poly[rows, :] = partial
            low_square[rows, :] = short(partial)
        for rows in panels:
            fourth[rows, :] = short(
                3.125 * poly[rows, :] - dot(low_square[rows, :], low_square[...])
            )
        for rows in panels:
            work[rows, :] = 2.44140625 * work[rows, :] - dot(fourth[rows, :], low[...])
        for rows in panels:
            low[rows, :] = short(work[rows, :])

    def apply_left():
        for rows in panels:
            total[rows, :] = 1.25 * total[rows, :] - dot(low[rows, :], short_total[...])
        for rows in panels:
            short_total[rows, :] = short(total[rows, :])

    def apply_right():
        for rows in panels:
            value = 1.25 * total[rows, :] - dot(short_total[rows, :], low[...])
            total[rows, :] = value
            short_total[rows, :] = short(value)

    def chain(count, apply):
        apply()

        @pl.when(count > 1)
        def _():
            advance()
            apply()

        @pl.when(count > 2)
        def _():
            advance()
            apply()

    left_scale = start(0, old_left, ((1,), (1,)))
    grad_square = jnp.zeros((1, 1), jnp.float32)
    for rows in panels:
        value = grad[rows, :].astype(jnp.float32)
        total[rows, :] = value
        grad_square = grad_square + jnp.sum(value * value, keepdims=True)
        short_total[rows, :] = grad[rows, :]
    chain(steps[2 * block], apply_left)
    right_scale = start(1, old_right, ((0,), (0,)))
    chain(steps[2 * block + 1], apply_right)
    cond_square = jnp.zeros((1, 1), jnp.float32)
    for rows in panels:
        value = total[rows, :] * (left_scale * right_scale)
        total[rows, :] = value
        cond_square = cond_square + jnp.sum(value * value, keepdims=True)
    half = short(total[pl.ds(pl.multiple_of((member & 1) * HALF, HALF), HALF), :])
    half_out[...] = half
    row = lax.broadcasted_iota(jnp.int32, (8, 128), 0)
    sums_out[...] = jnp.where(row < 4, cond_square, grad_square)


def refresh(position, steps, pieces):
    full = (ORDER, ORDER)
    return pl.pallas_call(
        refresh_kernel,
        out_shape=(
            jax.ShapeDtypeStruct((2, SLAB, ORDER), jnp.float32),
            jax.ShapeDtypeStruct((HALF, ORDER), jnp.bfloat16),
            jax.ShapeDtypeStruct((8, 128), jnp.float32),
        ),
        in_specs=[SMEM] * 2 + [VMEM] * 8,
        out_specs=(VMEM,) * 3,
        scratch_shapes=[pltpu.VMEM(full, jnp.bfloat16)] * 7 + [pltpu.VMEM(full, jnp.float32)] * 3,
        compiler_params=PARAMS,
        name="refresh",
    )(position, steps, *pieces)


def spread_kernel(half, mirrored, out):
    for column in range(COLUMNS):
        out[column, 0:HALF, :] = half[...]
        out[column, HALF:, :] = mirrored[...]


def spread(half, mirrored):
    return pl.pallas_call(
        spread_kernel,
        out_shape=jax.ShapeDtypeStruct((COLUMNS, ORDER, ORDER), jnp.bfloat16),
        in_specs=[VMEM] * 2,
        out_specs=VMEM,
        compiler_params=PARAMS,
        name="spread",
    )(half, mirrored)


def place_kernel(position, sums, *refs):
    sources, out, staged, sems = refs[:2], refs[2], refs[3], refs[4]
    ratio = jnp.sqrt(sums[4:5, 0:1] / (sums[0:1, 0:1] + epsilon))
    slot = ((position[0] // GROUP) & 1) * 2 + (position[0] & 1)
    stores = []
    for relative in range(4):
        first = relative // 2 * HALF
        for column in range(COLUMNS):
            index = relative * COLUMNS + column
            piece = sources[relative & 1][column, first : first + HALF]
            staged[index] = short(piece.astype(jnp.float32) * ratio)
            row = (column * 4 + (slot ^ relative)) * HALF
            rows = pl.ds(pl.multiple_of(row, HALF), HALF)
            store = pltpu.make_async_copy(staged.at[index], out.at[0, rows], sems.at[index])
            store.start()
            stores.append(store)
    for store in stores:
        store.wait()


def place(position, sums, sources):
    return pl.pallas_call(
        place_kernel,
        out_shape=jax.ShapeDtypeStruct((1, 4 * COLUMNS * HALF, ORDER), jnp.bfloat16),
        in_specs=[SMEM] + [VMEM] * 3,
        out_specs=HBM,
        scratch_shapes=[
            pltpu.VMEM((4 * COLUMNS, HALF, ORDER), jnp.bfloat16),
            pltpu.SemaphoreType.DMA((4 * COLUMNS,)),
        ],
        compiler_params=PARAMS,
        name="place",
    )(position, sums, *sources)


def per_device(grads, left_old, right_old, root_steps):
    position = jnp.reshape(lax.axis_index("dp"), (1,))
    steps = jnp.reshape(root_steps, (16,))
    part = lax.broadcasted_iota(jnp.int32, (3, 1, 1), 0)
    olds = jnp.where(part == 1, left_old, right_old)
    own = jnp.where(part == 0, grads, short(olds)).reshape(3 * SLAB, ORDER)
    far = flipped(own, "dp", 4)
    near = flipped(own, "dp", 2)
    far, steps = lax.optimization_barrier((far, steps))
    both = flipped(far, "dp", 2)
    pieces = [None] * 8
    for relative, piece in ((0, own), (2, near), (4, far), (6, both)):
        pieces[relative] = piece
        pieces[relative + 1] = flipped(piece, "dp", 1)
    products, half, sums = refresh(position, steps, pieces)
    left_rows = decay_rate * left_old + products[0:1]
    right_rows = decay_rate * right_old + products[1:2]

    columns = [[16 * i + k for i in range(COLUMNS)] for k in range(16)]
    mirrored = flipped(half, "dp", 14)
    for mask in (1, 2):
        sums = sums + flipped(sums, "shard", mask)
    mirrored, sums, left_rows, right_rows = lax.optimization_barrier(
        (mirrored, sums, left_rows, right_rows)
    )
    copies = spread(half, mirrored)
    mine = lax.all_to_all(copies, "dp", 0, 0, axis_index_groups=columns)
    sums = sums + flipped(sums, "shard", 7)
    for mask in (14, 16):
        sums = sums + flipped(sums, "dp", mask)
    mine, sums = lax.optimization_barrier((mine, sums))
    other = flipped(mine, "dp", 1)
    sums = sums + flipped(sums, "dp", 32)
    update = place(position, sums, [mine, other])
    return (update, left_rows, right_rows)


def solution(mesh):
    placed = (
        P("shard", "dp", None),
        P("shard", "dp", None),
        P("shard", "dp", None),
        P("shard", None, None),
    )
    return jax.shard_map(
        per_device,
        mesh=mesh,
        in_specs=placed,
        out_specs=(P("shard", None, None), P("shard", "dp", None), P("shard", "dp", None)),
        check_vma=False,
    )
```

```python
import jax
import jax.numpy as jnp
from jax import lax
from jax.experimental import pallas as pl
from jax.experimental.pallas import tpu as pltpu
from jax.sharding import PartitionSpec as P

GROUP = 8
SLAB = 64
ORDER = 512
HALF = ORDER // 2
PANEL = 256
COLUMNS = 4

epsilon = 1e-06
decay_rate = 0.95

VMEM = pl.BlockSpec(memory_space=pltpu.VMEM)
SMEM = pl.BlockSpec(memory_space=pltpu.SMEM)
HBM = pl.BlockSpec(memory_space=pltpu.HBM)
PARAMS = pltpu.CompilerParams(vmem_limit_bytes=16 * 1024 * 1024)


def flipped(value, axis, mask):
    return lax.ppermute(value, axis, [(i, i ^ mask) for i in range(lax.axis_size(axis))])


def dot(left, right, dims=((1,), (0,))):
    return lax.dot_general(left, right, (dims, ((), ())), preferred_element_type=jnp.float32)


def short(value):
    return value.astype(jnp.bfloat16)


def refresh_kernel(position, steps, *refs):
    pieces = refs[:8]
    products_out, half_out, sums_out = refs[8:11]
    grad, old_left, old_right, low, low_square, fourth, short_total, work, poly, total = refs[11:]
    member = position[0] & (GROUP - 1)
    block = position[0] // GROUP
    for relative, piece in enumerate(pieces):
        rows = pl.ds(pl.multiple_of((member ^ relative) * SLAB, SLAB), SLAB)
        grad[rows, :] = piece[0:SLAB, :]
        old_left[rows, :] = piece[SLAB : 2 * SLAB, :]
        old_right[rows, :] = piece[2 * SLAB :, :]
    own = pl.ds(pl.multiple_of(member * SLAB, SLAB), SLAB)

    panels = [pl.ds(row, PANEL) for row in range(0, ORDER, PANEL)]

    def start(side, old, dims):
        square = jnp.zeros((1, 1), jnp.float32)
        for rows in panels:
            if side == 0:
                product = dot(grad[rows, :], grad[...], dims)
            else:
                product = dot(grad[:, rows], grad[...], dims)
            work[rows, :] = product
            factor = product + decay_rate * old[rows, :].astype(jnp.float32)
            poly[rows, :] = factor
            square = square + jnp.sum(factor * factor, keepdims=True)
        products_out[side] = work[own, :]
        scaling = 2.5 / jnp.sqrt(square + epsilon)
        for rows in panels:
            quarter = poly[rows, :] * (scaling * 0.25)
            work[rows, :] = quarter
            low[rows, :] = short(quarter)
        return jnp.sqrt(jnp.sqrt(scaling))

    def advance():
        for rows in panels:
            partial = 2.5 * work[rows, :] - dot(low[rows, :], low[...])
            poly[rows, :] = partial
            low_square[rows, :] = short(partial)
        for rows in panels:
            fourth[rows, :] = short(
                3.125 * poly[rows, :] - dot(low_square[rows, :], low_square[...])
            )
        for rows in panels:
            work[rows, :] = 2.44140625 * work[rows, :] - dot(fourth[rows, :], low[...])
        for rows in panels:
            low[rows, :] = short(work[rows, :])

    def apply_left():
        for rows in panels:
            total[rows, :] = 1.25 * total[rows, :] - dot(low[rows, :], short_total[...])
        for rows in panels:
            short_total[rows, :] = short(total[rows, :])

    def apply_right():
        for rows in panels:
            value = 1.25 * total[rows, :] - dot(short_total[rows, :], low[...])
            total[rows, :] = value
            short_total[rows, :] = short(value)

    def chain(count, apply):
        apply()

        @pl.when(count > 1)
        def _():
            advance()
            apply()

        @pl.when(count > 2)
        def _():
            advance()
            apply()

    left_scale = start(0, old_left, ((1,), (1,)))
    grad_square = jnp.zeros((1, 1), jnp.float32)
    for rows in panels:
        value = grad[rows, :].astype(jnp.float32)
        total[rows, :] = value
        grad_square = grad_square + jnp.sum(value * value, keepdims=True)
        short_total[rows, :] = grad[rows, :]
    chain(steps[2 * block], apply_left)
    right_scale = start(1, old_right, ((0,), (0,)))
    chain(steps[2 * block + 1], apply_right)
    cond_square = jnp.zeros((1, 1), jnp.float32)
    for rows in panels:
        value = total[rows, :] * (left_scale * right_scale)
        total[rows, :] = value
        cond_square = cond_square + jnp.sum(value * value, keepdims=True)
    half = short(total[pl.ds(pl.multiple_of((member & 1) * HALF, HALF), HALF), :])
    half_out[...] = half
    row = lax.broadcasted_iota(jnp.int32, (8, 128), 0)
    sums_out[...] = jnp.where(row < 4, cond_square, grad_square)


def refresh(position, steps, pieces):
    full = (ORDER, ORDER)
    return pl.pallas_call(
        refresh_kernel,
        out_shape=(
            jax.ShapeDtypeStruct((2, SLAB, ORDER), jnp.float32),
            jax.ShapeDtypeStruct((HALF, ORDER), jnp.bfloat16),
            jax.ShapeDtypeStruct((8, 128), jnp.float32),
        ),
        in_specs=[SMEM] * 2 + [VMEM] * 8,
        out_specs=(VMEM,) * 3,
        scratch_shapes=[pltpu.VMEM(full, jnp.bfloat16)] * 7 + [pltpu.VMEM(full, jnp.float32)] * 3,
        compiler_params=PARAMS,
        name="refresh",
    )(position, steps, *pieces)


def spread_kernel(half, mirrored, out, sems):
    copies = []
    for column in range(COLUMNS):
        for side, source in enumerate((half, mirrored)):
            rows = pl.ds(side * HALF, HALF)
            copy = pltpu.make_async_copy(source, out.at[column, rows], sems.at[2 * column + side])
            copy.start()
            copies.append(copy)
    for copy in copies:
        copy.wait()


def spread(half, mirrored):
    return pl.pallas_call(
        spread_kernel,
        out_shape=jax.ShapeDtypeStruct((COLUMNS, ORDER, ORDER), jnp.bfloat16),
        in_specs=[VMEM] * 2,
        out_specs=HBM,
        scratch_shapes=[pltpu.SemaphoreType.DMA((2 * COLUMNS,))],
        compiler_params=PARAMS,
        name="spread",
    )(half, mirrored)


def place_kernel(position, sums, *refs):
    sources, out, staged, sems = refs[:2], refs[2], refs[3], refs[4]
    ratio = jnp.sqrt(sums[4:5, 0:1] / (sums[0:1, 0:1] + epsilon))
    slot = ((position[0] // GROUP) & 1) * 2 + (position[0] & 1)
    stores = []
    for relative in range(4):
        first = relative // 2 * HALF
        for column in range(COLUMNS):
            index = relative * COLUMNS + column
            piece = sources[relative & 1][column, first : first + HALF]
            staged[index] = short(piece.astype(jnp.float32) * ratio)
            row = (column * 4 + (slot ^ relative)) * HALF
            rows = pl.ds(pl.multiple_of(row, HALF), HALF)
            store = pltpu.make_async_copy(staged.at[index], out.at[0, rows], sems.at[index])
            store.start()
            stores.append(store)
    for store in stores:
        store.wait()


def place(position, sums, sources):
    return pl.pallas_call(
        place_kernel,
        out_shape=jax.ShapeDtypeStruct((1, 4 * COLUMNS * HALF, ORDER), jnp.bfloat16),
        in_specs=[SMEM] + [VMEM] * 3,
        out_specs=HBM,
        scratch_shapes=[
            pltpu.VMEM((4 * COLUMNS, HALF, ORDER), jnp.bfloat16),
            pltpu.SemaphoreType.DMA((4 * COLUMNS,)),
        ],
        compiler_params=PARAMS,
        name="place",
    )(position, sums, *sources)


def per_device(grads, left_old, right_old, root_steps):
    position = jnp.reshape(lax.axis_index("dp"), (1,))
    steps = jnp.reshape(root_steps, (16,))
    part = lax.broadcasted_iota(jnp.int32, (3, 1, 1), 0)
    olds = jnp.where(part == 1, left_old, right_old)
    own = jnp.where(part == 0, grads, short(olds)).reshape(3 * SLAB, ORDER)
    far = flipped(own, "dp", 4)
    near = flipped(own, "dp", 2)
    far, steps = lax.optimization_barrier((far, steps))
    both = flipped(far, "dp", 2)
    pieces = [None] * 8
    for relative, piece in ((0, own), (2, near), (4, far), (6, both)):
        pieces[relative] = piece
        pieces[relative + 1] = flipped(piece, "dp", 1)
    products, half, sums = refresh(position, steps, pieces)
    left_rows = decay_rate * left_old + products[0:1]
    right_rows = decay_rate * right_old + products[1:2]

    columns = [[16 * i + k for i in range(COLUMNS)] for k in range(16)]
    mirrored = flipped(half, "dp", 14)
    for mask in (1, 2):
        sums = sums + flipped(sums, "shard", mask)
    mirrored, sums, left_rows, right_rows = lax.optimization_barrier(
        (mirrored, sums, left_rows, right_rows)
    )
    copies = spread(half, mirrored)
    mine = lax.all_to_all(copies, "dp", 0, 0, axis_index_groups=columns)
    sums = sums + flipped(sums, "shard", 7)
    for mask in (14, 16):
        sums = sums + flipped(sums, "dp", mask)
    mine, sums = lax.optimization_barrier((mine, sums))
    other = flipped(mine, "dp", 1)
    sums = sums + flipped(sums, "dp", 32)
    update = place(position, sums, [mine, other])
    return (update, left_rows, right_rows)


def solution(mesh):
    placed = (
        P("shard", "dp", None),
        P("shard", "dp", None),
        P("shard", "dp", None),
        P("shard", None, None),
    )
    return jax.shard_map(
        per_device,
        mesh=mesh,
        in_specs=placed,
        out_specs=(P("shard", None, None), P("shard", "dp", None), P("shard", "dp", None)),
        check_vma=False,
    )
```
